32 devices in a mesh: grp: 2 (over x), row: 16 (over z, y, core).
Axes of the slice: x: 2, y: 2, z: 4, core: 2. Of those that a mesh axis runs over, the one named last changes fastest.
Arguments:
- features: bfloat16 [16384, 768], P(('grp', 'row')), parts along dimension 0, may hold values from -6 to 6
- degree: int32 [16384], P(('grp', 'row')), parts along dimension 0, may hold values from 8 to 63
- block_list: int32 [576, 2], P(('grp', 'row')), parts along dimension 0, may hold values from 0 to 31, as said below
- block_count: int32 [32], P(('grp', 'row')), parts along dimension 0, may hold values from 12 to 18, as said below
- tiles: bfloat16 [576, 256, 256], P(('grp', 'row')), parts along dimension 0, may hold values from 0 to 1
- self_weight: bfloat16 [768, 512], replicated, may hold values from -0.21875 to 0.21875
- neigh_weight: bfloat16 [768, 512], replicated, may hold values from -0.21875 to 0.21875
- bias: float32 [512], replicated, may hold values from -3 to 3
- cotangent: bfloat16 [16384, 512], P(('grp', 'row')), parts along dimension 0, may hold values from -6 to 6
Outputs:
- activated: bfloat16 [16384, 512], P(('grp', 'row')), parts along dimension 0
- grad_features: bfloat16 [16384, 768], P(('grp', 'row')), parts along dimension 0
- grad_self: float32 [1536, 512], P('grp'), parts along dimension 0
- grad_neigh: float32 [1536, 512], P('grp'), parts along dimension 0
- grad_bias: float32 [1024], P('grp'), parts along dimension 0
The draws below stay inside these ranges and needn't reach their ends.
There are 2 independent parts, one for each index of `grp`. The reference program is written for one: setup_inputs(seed, part) draws one part's arguments, and reference() takes and returns one part's arrays. A program takes and returns all parts, laid end to end along the dimension named above; an argument that names none is the same for every part. Nothing has to cross between parts.
Inputs may be any that keep to these rules, and one draw needn't show every extreme that they name: `block_list`: column 0 of a slot is a row tile among the 2 tile rows of the device that holds the slot; column 1 is a column tile among the tile rows of the devices up to 4 away along row, counted cyclically over 32 tile rows. The 18 slots of a device name distinct column tiles, so all of them together cover that device's whole reach. `block_count`: the live slots of a device are its leading ones; some device has all 18 live.
All inputs are finite; a program needn't handle non-finite values.
Results may differ from the reference program's by a relative error of at most 0.0059.
Values may be sent and summed in bfloat16 or wider, within the bound.
A program may use at most 64 MiB of HBM per device.

```python
import jax
import jax.numpy as jnp
from jax import lax

F_IN = 768
HID = 512
TILE = 256
HOPS = 4
TROWS = 2
BLK_DEV = 18
TILES = 32
NODES = 8192
BLOCKS = 288
N_ROW = 16


def draw_block_list(key, part):
    key = jax.random.fold_in(key, 1)
    row_key, perm_key = jax.random.split(key)
    span = (2 * HOPS + 1) * TROWS
    device_keys = jax.random.split(perm_key, N_ROW)
    orders = jax.vmap(lambda one_key: jax.random.permutation(one_key, span))(device_keys).astype(jnp.int32)
    offset = orders.reshape(BLOCKS) - HOPS * TROWS
    device_of = jnp.arange(BLOCKS, dtype=jnp.int32) // BLK_DEV
    row_slot = jax.random.randint(row_key, (BLOCKS,), 0, TROWS, dtype=jnp.int32)
    row_tile = device_of * TROWS + row_slot
    col_tile = (device_of * TROWS + offset) % TILES
    return jnp.stack([row_tile, col_tile], axis=1).astype(jnp.int32)


def draw_block_count(key, part):
    key = jax.random.fold_in(key, 2)
    count_key, full_key = jax.random.split(key)
    lowest = (2 * BLK_DEV + 2) // 3
    counts = jax.random.randint(count_key, (N_ROW,), lowest, BLK_DEV + 1, dtype=jnp.int32)
    fullest = jax.random.randint(full_key, (), 0, N_ROW, dtype=jnp.int32)
    return jnp.where(jnp.arange(N_ROW, dtype=jnp.int32) == fullest, BLK_DEV, counts).astype(jnp.int32)


def with_ends(entries, key, smallest, high):
    spot = [jax.random.randint(jax.random.fold_in(key, axis), (), 0, length) for axis, length in enumerate(entries.shape)]
    widest = entries.shape.index(max(entries.shape))
    neighbour = spot[:widest] + [(spot[widest] + 1) % entries.shape[widest]] + spot[widest + 1:]
    return entries.at[tuple(spot)].set(smallest).at[tuple(neighbour)].set(high)


def block_levels(own_key, shape, cuts, smallest, top_value):
    loudness = 1.0
    for dim, shards_of in cuts:
        steps = jax.random.uniform(jax.random.fold_in(jax.random.fold_in(own_key, 6), dim), (shards_of,), jnp.float32, smallest / len(cuts), top_value / len(cuts))
        loudness = loudness * jnp.repeat(jnp.exp(steps), shape[dim] // shards_of).reshape((-1,) + (1,) * (len(shape) - 1 - dim))
    return loudness


def noise(stream_key, dims, scale, most, shards=(), kind=jnp.bfloat16):
    level = block_levels(stream_key, dims, shards, -0.22, 0.18) if shards else 1.0
    drawn = jax.random.normal(stream_key, dims, jnp.float32) * scale * level
    return jnp.minimum(jnp.maximum(drawn, -most), most).astype(kind)


def setup_inputs(seed: int = 0, part: int = 0) -> dict:
    arg_keys = jax.random.split(jax.random.key(seed), 10)
    part_splits = jax.random.split(jax.random.fold_in(arg_keys[9], part), 10)
    features = noise(part_splits[0], (NODES, F_IN), 1.0, 6.0, ((0, 16),))
    degree = with_ends(jax.random.randint(part_splits[1], (NODES,), 8, 64), jax.random.fold_in(part_splits[1], 1), 8, 63).astype(jnp.int32)
    block_list = draw_block_list(jax.random.fold_in(jax.random.fold_in(arg_keys[9], part), 71), part)
    block_count = draw_block_count(jax.random.fold_in(jax.random.fold_in(arg_keys[9], part), 71), part)
    tiles = jnp.clip(1.0 * jax.random.uniform(part_splits[4], (BLOCKS, TILE, TILE), jnp.float32) ** block_levels(part_splits[4], (BLOCKS, TILE, TILE), ((0, 16),), -0.2, 0.2), 0.0, 1.0).astype(jnp.bfloat16)
    self_weight = noise(arg_keys[5], (F_IN, HID), F_IN ** -0.5, 0.21875)
    neigh_weight = noise(arg_keys[6], (F_IN, HID), F_IN ** -0.5, 0.21875)
    bias = noise(arg_keys[7], (HID,), 0.5, 3.0, (), jnp.float32)
    cotangent = noise(part_splits[8], (NODES, HID), 1.0, 6.0, ((0, 16),))
    return dict(features=features, degree=degree, block_list=block_list, block_count=block_count, tiles=tiles, self_weight=self_weight, neigh_weight=neigh_weight, bias=bias, cotangent=cotangent)


def smooth_gate(values):
    return jax.nn.gelu(values, approximate=True)

def reference(features, degree, block_list, block_count, tiles, self_weight, neigh_weight, bias, cotangent):
    projected = jnp.dot(features, neigh_weight, preferred_element_type=jnp.float32).astype(jnp.bfloat16)

    def forward_block(block, gathered):
        active = block % BLK_DEV < block_count[block // BLK_DEV]
        row_start = (block_list[block, 0] * TILE).astype(jnp.int32)
        col_start = (block_list[block, 1] * TILE).astype(jnp.int32)

        def apply(current):
            source = lax.dynamic_slice_in_dim(projected, col_start, TILE, 0)
            partial_value = jnp.dot(tiles[block], source, preferred_element_type=jnp.float32)
            target = lax.dynamic_slice_in_dim(current, row_start, TILE, 0)
            return lax.dynamic_update_slice_in_dim(current, target + partial_value, row_start, 0)

        def keep(current):
            return current
        return lax.cond(active, apply, keep, gathered)
    summed = lax.fori_loop(0, BLOCKS, forward_block, jnp.zeros((NODES, HID), jnp.float32))
    scale = degree.astype(jnp.float32)[:, None]
    pre = jnp.dot(features, self_weight, preferred_element_type=jnp.float32) + summed / scale + bias[None, :]
    activated, pullback = jax.vjp(smooth_gate, pre)
    grad_pre = pullback(cotangent.astype(jnp.float32))[0]
    message = (grad_pre / scale).astype(jnp.bfloat16)

    def backward_block(block, gathered):
        active = block % BLK_DEV < block_count[block // BLK_DEV]
        row_start = (block_list[block, 0] * TILE).astype(jnp.int32)
        col_start = (block_list[block, 1] * TILE).astype(jnp.int32)

        def apply(current):
            source = lax.dynamic_slice_in_dim(message, row_start, TILE, 0)
            partial_value = lax.dot_general(tiles[block], source, (((0,), (0,)), ((), ())), preferred_element_type=jnp.float32)
            target = lax.dynamic_slice_in_dim(current, col_start, TILE, 0)
            return lax.dynamic_update_slice_in_dim(current, target + partial_value, col_start, 0)

        def keep(current):
            return current
        return lax.cond(active, apply, keep, gathered)
    grad_proj = lax.fori_loop(0, BLOCKS, backward_block, jnp.zeros((NODES, HID), jnp.float32))
    grad_pre_b = grad_pre.astype(jnp.bfloat16)
    grad_proj_b = grad_proj.astype(jnp.bfloat16)
    contract_out = (((1,), (1,)), ((), ()))
    grad_features = (lax.dot_general(grad_pre_b, self_weight, contract_out, preferred_element_type=jnp.float32) + lax.dot_general(grad_proj_b, neigh_weight, contract_out, preferred_element_type=jnp.float32)).astype(jnp.bfloat16)
    contract_rows = (((0,), (0,)), ((), ()))
    grad_self = lax.dot_general(features, grad_pre_b, contract_rows, preferred_element_type=jnp.float32)
    grad_neigh = lax.dot_general(features, grad_proj_b, contract_rows, preferred_element_type=jnp.float32)
    grad_bias = lax.optimization_barrier(jnp.sum(grad_pre, axis=0))
    return (activated.astype(jnp.bfloat16), grad_features, grad_self, grad_neigh, grad_bias)
```

```python
import functools

import jax
import jax.numpy as jnp
from jax import lax
from jax.experimental import pallas as pl
from jax.experimental.pallas import tpu as pltpu
from jax.sharding import PartitionSpec as P

MESH = pl.DeviceIdType.MESH
F32 = jnp.float32
BF16 = jnp.bfloat16
CHUNKS = 4
NEAR = 9
TANH_SCALE = 0.7978845608028654
TANH_CUBE = 0.044715


def dot(a, b):
    return jnp.dot(a, b, preferred_element_type=F32)


def dot_nt(a, b):
    return lax.dot_general(a, b, (((1,), (1,)), ((), ())), preferred_element_type=F32)


def kernel(
    n_row,
    reduce_here,
    feat,
    degree,
    blist,
    bcount,
    tiles,
    w_self,
    w_neigh,
    bias,
    cot,
    act_out,
    gfeat_out,
    gself_out,
    gneigh_out,
    gbias_out,
    win,
    dense,
    dense_t,
    feat_t,
    acc,
    gpre_b,
    msg,
    lane_out,
    lane_in,
    net_out,
    net_in,
    gloc,
    tab,
    fsend,
    frecv,
    lsend,
    lrecv,
    nsend,
    nrecv,
    *red
):
    row = lax.axis_index("row")
    core = lax.rem(row, 2)
    chip = row // 2
    chips = n_row // 2
    side = lax.rem(chip, 2)
    sgn = 2 * side - 1

    def at(chip_off, c):
        return lax.rem(chip + chip_off + 4 * chips, chips) * 2 + c

    other = 1 - core
    partner = at(0, other)
    ypair = at(-sgn, core)
    zpos = at(2 * sgn, core)
    zneg = at(-2 * sgn, core)
    greet = [partner, ypair, zpos, zneg]
    if reduce_here:
        zline = [at(2 * j, core) for j in range(1, chips // 2)]
        greet = [partner, ypair] + zline

    def rc(src, dst, ssem, rsem, dev):
        return pltpu.make_async_remote_copy(
            src_ref=src,
            dst_ref=dst,
            send_sem=ssem,
            recv_sem=rsem,
            device_id={"row": dev},
            device_id_type=MESH,
        )

    barrier = pltpu.get_barrier_semaphore()
    for dev in greet:
        pl.semaphore_signal(barrier, inc=1, device_id={"row": dev}, device_id_type=MESH)
    pl.semaphore_wait(barrier, len(greet))

    nodes = feat.shape[0]
    tile = tiles.shape[1]
    step = nodes // CHUNKS

    def rows_of(ch):
        return pl.ds(pl.multiple_of(ch * step, step), step)

    def loop(count, body):
        def run(i, carry):
            body(i)
            return carry

        lax.fori_loop(0, count, run, 0)

    far = 3 + lax.rem(core + side, 2)
    own_sends = ((0, 3, zpos), (1, 4, zneg), (2, 2, ypair), (3, 1, partner))

    def fcopy(i, src, dst, ch, dev):
        rows = rows_of(ch)
        return rc(win.at[src, rows], win.at[dst, rows], fsend.at[i, ch], frecv.at[dst, ch], dev)

    def fwait(slot, ch):
        fcopy(0, slot, slot, ch, partner).wait_recv()

    def project(ch):
        rows = rows_of(ch)
        win[0, rows, :] = dot(feat[rows, :], w_neigh[...]).astype(BF16)
        for i, dst, dev in own_sends:
            fcopy(i, 0, dst, ch, dev).start()

    loop(CHUNKS, project)

    devs = (
        at(0, core),
        at(0, other),
        at(-sgn, core),
        at(-2 * sgn, core),
        at(2 * sgn, core),
        at(-sgn, other),
        at(2 * (2 * core - 1), other),
        at(sgn, core),
        at(sgn, other),
    )
    for b, dev in enumerate(devs):
        tab[b] = dev
    slots = tiles.shape[0]

    def densify(b):
        for t in range(2):
            column = tab[b] * 2 + t

            def seek(j, found):
                return jnp.maximum(found, jnp.where(blist[j, 1] == column, j, 0))

            slot = lax.fori_loop(0, slots, seek, 0)
            target = blist[slot, 0] - 2 * row
            live = slot < bcount[0]
            block = tiles[slot]
            flipped = block.T
            for r in range(2):
                take = jnp.logical_and(live, target == r)
                here = pl.ds(r * tile, tile)
                there = pl.ds(t * tile, tile)
                dense[b, here, there] = jnp.where(take, block, jnp.zeros_like(block))
                dense_t[b, there, here] = jnp.where(take, flipped, jnp.zeros_like(flipped))

    loop(NEAR, densify)

    def self_part(ch):
        rows = rows_of(ch)
        acc[rows, :] = dot(dense[0, rows, :], win[0])

    loop(CHUNKS, self_part)

    def add_block(b):
        def body(ch):
            rows = rows_of(ch)
            acc[rows, :] += dot(dense[b, rows, :], win[b])

        loop(CHUNKS, body)

    def relay(ch):
        fwait(3, ch)
        fcopy(4, 3, 7, ch, ypair).start()
        fwait(2, ch)
        fcopy(5, 2, 5, ch, partner).start()
        fwait(4, ch)
        fcopy(6, far, 6, ch, partner).start()

    loop(CHUNKS, relay)
    feat_t[...] = feat[...].T

    def arrive(b):
        loop(CHUNKS, lambda ch: fwait(b, ch))
        add_block(b)

    arrive(1)
    add_block(2)
    add_block(3)
    add_block(4)
    arrive(5)
    arrive(6)

    def relay_on(ch):
        fwait(7, ch)
        fcopy(7, 7, 8, ch, partner).start()

    loop(CHUNKS, relay_on)
    add_block(7)
    arrive(8)

    bias_rows = 8

    def activate(ch, bias_sum):
        rows = rows_of(ch)
        inverse = 1.0 / degree[rows, :].astype(F32)
        pre = dot(feat[rows, :], w_self[...]) + acc[rows, :] * inverse + bias[...]
        square = pre * pre
        t = jnp.tanh(TANH_SCALE * (pre + TANH_CUBE * (square * pre)))
        half = 0.5 * (1.0 + t)
        act_out[rows, :] = (pre * half).astype(BF16)
        slope = half + (0.5 * TANH_SCALE) * pre * (1.0 - t * t) * (1.0 + (3.0 * TANH_CUBE) * square)
        grad_pre = cot[rows, :].astype(F32) * slope
        gpre_b[rows, :] = grad_pre.astype(BF16)
        msg[rows, :] = (grad_pre * inverse).astype(BF16)
        return bias_sum + jnp.sum(
            grad_pre.reshape(step // bias_rows, bias_rows, grad_pre.shape[1]), axis=0
        )

    bias_sum = lax.fori_loop(0, CHUNKS, activate, jnp.zeros((bias_rows, acc.shape[1]), F32))

    def term(b, rows):
        return dot(dense_t[b, rows, :], msg[...])

    def lcopy(i, ch):
        rows = rows_of(ch)
        return rc(lane_out.at[i, rows], lane_in.at[i, rows], lsend.at[i, ch], lrecv.at[i, ch], partner)

    def ncopy(i, ch, dev):
        rows = rows_of(ch)
        return rc(net_out.at[i, rows], net_in.at[i, rows], nsend.at[i, ch], nrecv.at[i, ch], dev)

    def lane_term(i, b):
        def body(ch):
            rows = rows_of(ch)
            lane_out[i, rows, :] = term(b, rows).astype(BF16)
            lcopy(i, ch).start()

        return body

    loop(CHUNKS, lane_term(0, 8))
    loop(CHUNKS, lane_term(1, 6))

    def send_relay(ch):
        rows = rows_of(ch)
        mine = term(7, rows)
        lcopy(0, ch).wait_recv()
        net_out[0, rows, :] = (mine + lane_in[0, rows, :].astype(F32)).astype(BF16)
        ncopy(0, ch, ypair).start()

    loop(CHUNKS, send_relay)
    far_pos = (core != side).astype(F32)
    far_neg = 1.0 - far_pos

    def send_pos(ch):
        rows = rows_of(ch)
        mine = term(4, rows)
        lcopy(1, ch).wait_recv()
        net_out[1, rows, :] = (mine + far_pos * lane_in[1, rows, :].astype(F32)).astype(BF16)
        ncopy(1, ch, zpos).start()

    loop(CHUNKS, send_pos)
    loop(CHUNKS, lane_term(2, 5))

    def send_y(ch):
        rows = rows_of(ch)
        mine = term(2, rows)
        lcopy(2, ch).wait_recv()
        net_out[2, rows, :] = (mine + lane_in[2, rows, :].astype(F32)).astype(BF16)
        ncopy(2, ch, ypair).start()

    loop(CHUNKS, send_y)

    def send_neg(ch):
        rows = rows_of(ch)
        mine = term(3, rows) + far_neg * lane_in[1, rows, :].astype(F32)
        ncopy(0, ch, ypair).wait_recv()
        net_out[3, rows, :] = (mine + net_in[0, rows, :].astype(F32)).astype(BF16)
        ncopy(3, ch, zneg).start()

    loop(CHUNKS, send_neg)
    loop(CHUNKS, lane_term(3, 1))

    f_in = feat.shape[1]
    half_f, quarter_f = f_in // 2, f_in // 4
    f_step = f_in // CHUNKS

    def weight_grad(g, source):
        def body(i):
            rows = pl.ds(pl.multiple_of(i * f_step, f_step), f_step)
            gloc[g, rows, :] = dot(feat_t[rows, :], source[...])

        loop(CHUNKS, body)

    weight_grad(0, gpre_b)

    if reduce_here:
        (s1, r1, s2, r2, s3, r3, gath, b_out, b_in, gs, gr, bs, br) = red
        depth = chips // 2
        piece_f = quarter_f // depth
        z = chip // 2
        my_half = pl.multiple_of(core * half_f, half_f)
        not_half = pl.multiple_of(other * half_f, half_f)
        my_quarter = pl.multiple_of(my_half + side * quarter_f, quarter_f)
        not_quarter = pl.multiple_of(my_half + (1 - side) * quarter_f, quarter_f)
        my_piece = pl.multiple_of(my_quarter + z * piece_f, piece_f)
        far_z = [lax.rem(z + j, depth) for j in range(1, depth)]

        def c1(g):
            return rc(s1.at[g], r1.at[g], gs.at[g, 0], gr.at[g, 0], partner)

        def c2(g):
            return rc(s2.at[g], r2.at[g], gs.at[g, 1], gr.at[g, 1], ypair)

        def c3(g, j):
            return rc(
                s3.at[g, far_z[j]], r3.at[g, j], gs.at[g, 2 + j], gr.at[g, 2 + j], zline[j]
            )

        def c4(g, j, mine=True):
            z_of = z if mine else lax.rem(z + depth - 1 - j, depth)
            ref = gath.at[g, core, side, z_of]
            return rc(ref, ref, gs.at[g, 1 + depth + j], gr.at[g, 1 + depth + j], zline[j])

        last = 2 * depth

        def c5(g, mine=True):
            ref = gath.at[g, core, side if mine else 1 - side]
            return rc(ref, ref, gs.at[g, last], gr.at[g, last], ypair)

        def c6(g, mine=True):
            ref = gath.at[g, core if mine else other]
            return rc(ref, ref, gs.at[g, last + 1], gr.at[g, last + 1], partner)

        def stage1(g):
            s1[g] = gloc[g, pl.ds(not_half, half_f), :].astype(BF16)
            c1(g).start()

        def stage2(g):
            c1(g).wait_recv()
            skip = pl.multiple_of((1 - side) * quarter_f, quarter_f)
            s2[g] = (
                gloc[g, pl.ds(not_quarter, quarter_f), :]
                + r1[g, pl.ds(skip, quarter_f), :].astype(F32)
            ).astype(BF16)
            c2(g).start()

        def stage3(g):
            keep = pl.multiple_of(side * quarter_f, quarter_f)
            mine = (
                gloc[g, pl.ds(my_quarter, quarter_f), :]
                + r1[g, pl.ds(keep, quarter_f), :].astype(F32)
            )
            c2(g).wait_recv()
            mine = mine + r2[g].astype(F32)
            gloc[g, pl.ds(my_quarter, quarter_f), :] = mine
            s3[g] = mine.astype(BF16).reshape(s3.shape[1:])
            for j in range(depth - 1):
                c3(g, j).start()

        def stage4(g):
            total = gloc[g, pl.ds(my_piece, piece_f), :]
            for j in range(depth - 1):
                c3(g, j).wait_recv()
                total = total + r3[g, j].astype(F32)
            gath[g, core, side, z] = total.astype(BF16)
            for j in range(depth - 1):
                c4(g, j).start()

        def stage5(g):
            for j in range(depth - 1):
                c4(g, j, False).wait_recv()
            c5(g).start()

        def stage6(g):
            c5(g, False).wait_recv()
            c6(g).start()

        def stage7(g, out):
            c6(g, False).wait_recv()
            out[...] = gath[g].astype(F32).reshape(out.shape)

        def bcopy(i, src, dev):
            return rc(b_out.at[src], b_in.at[i], bs.at[i], br.at[i], dev)

        b_out[0] = bias_sum
        bcopy(0, 0, partner).start()
        stage1(0)
        bcopy(0, 0, partner).wait_recv()
        b_out[1] = b_out[0] + b_in[0]
        bcopy(1, 1, ypair).start()
        stage2(0)
        bcopy(1, 1, ypair).wait_recv()
        b_out[2] = b_out[1] + b_in[1]
        for j in range(depth - 1):
            bcopy(2 + j, 2, zline[j]).start()

    g_rows = nodes // CHUNKS

    def feature_grad(ch):
        rows = rows_of(ch)
        gfeat_out[rows, :] = dot_nt(gpre_b[rows, :], w_self[...]).astype(BF16)

    def gather_own(ch):
        rows = rows_of(ch)
        total = term(0, rows)
        lcopy(3, ch).wait_recv()
        total = total + lane_in[3, rows, :].astype(F32)
        ncopy(2, ch, ypair).wait_recv()
        total = total + net_in[2, rows, :].astype(F32)
        ncopy(1, ch, zpos).wait_recv()
        total = total + net_in[1, rows, :].astype(F32)
        ncopy(3, ch, zneg).wait_recv()
        total = total + net_in[3, rows, :].astype(F32)
        msg_back[rows, :] = total.astype(BF16)

    msg_back = win.at[0]
    if reduce_here:
        stage3(0)
        stage4(0)
    for i, src, dst in ((0, 0, 3), (1, 0, 4), (2, 0, 2), (3, 0, 1), (4, 3, 7), (5, 2, 5), (6, 3, 6), (7, 7, 8)):
        loop(CHUNKS, lambda ch, i=i, src=src, dst=dst: fcopy(i, src, dst, ch, partner).wait_send())
    loop(CHUNKS, gather_own)
    weight_grad(1, msg_back)
    if reduce_here:
        stage1(1)
        stage5(0)
        stage2(1)
        stage6(0)
        stage3(1)

    def feature_grad(ch):
        rows = rows_of(ch)
        gfeat_out[rows, :] = (
            dot_nt(gpre_b[rows, :], w_self[...]) + dot_nt(msg_back[rows, :], w_neigh[...])
        ).astype(BF16)

    loop(CHUNKS, feature_grad)
    if reduce_here:
        stage4(1)
        stage7(0, gself_out)
        total = b_out[2]
        for j in range(depth - 1):
            bcopy(2 + j, 2, zline[j]).wait_recv()
            total = total + b_in[2 + j]
        gbias_out[...] = jnp.sum(total, axis=0, keepdims=True)
        stage5(1)
        stage6(1)
        stage7(1, gneigh_out)
        for g in range(2):
            c1(g).wait_send()
            c2(g).wait_send()
            for j in range(depth - 1):
                c3(g, j).wait_send()
                c4(g, j).wait_send()
            c5(g).wait_send()
            c6(g).wait_send()
        bcopy(0, 0, partner).wait_send()
        bcopy(1, 1, ypair).wait_send()
        for j in range(depth - 1):
            bcopy(2 + j, 2, zline[j]).wait_send()
    else:
        gself_out[...] = gloc[0]
        gneigh_out[...] = gloc[1]
        gbias_out[...] = jnp.sum(bias_sum, axis=0, keepdims=True)

    def drain(ch):
        for i in range(4):
            lcopy(i, ch).wait_send()
        for i, dev in enumerate((ypair, zpos, ypair, zneg)):
            ncopy(i, ch, dev).wait_send()

    loop(CHUNKS, drain)


def on_device(
    features, degree, block_list, block_count, tiles, self_weight, neigh_weight, bias, cotangent
):
    nodes, f_in = features.shape
    hid = neigh_weight.shape[1]
    n_row = lax.axis_size("row")
    depth = n_row // 4
    reduce_here = False
    vmem = pl.BlockSpec(memory_space=pltpu.VMEM)
    smem = pl.BlockSpec(memory_space=pltpu.SMEM)
    dma = pltpu.SemaphoreType.DMA
    block = (nodes, hid)
    scratch = [
        pltpu.VMEM((NEAR,) + block, BF16),
        pltpu.VMEM((NEAR, nodes, nodes), BF16),
        pltpu.VMEM((NEAR, nodes, nodes), BF16),
        pltpu.VMEM((f_in, nodes), BF16),
        pltpu.VMEM(block, F32),
        pltpu.VMEM(block, BF16),
        pltpu.VMEM(block, BF16),
        pltpu.VMEM((4,) + block, BF16),
        pltpu.VMEM((4,) + block, BF16),
        pltpu.VMEM((4,) + block, BF16),
        pltpu.VMEM((4,) + block, BF16),
        pltpu.VMEM((2, f_in, hid), F32),
        pltpu.SMEM((NEAR,), jnp.int32),
        dma((8, CHUNKS)),
        dma((NEAR, CHUNKS)),
        dma((4, CHUNKS)),
        dma((4, CHUNKS)),
        dma((4, CHUNKS)),
        dma((4, CHUNKS)),
    ]
    if reduce_here:
        half, quarter = f_in // 2, f_in // 4
        scratch += [
            pltpu.VMEM((2, half, hid), BF16),
            pltpu.VMEM((2, half, hid), BF16),
            pltpu.VMEM((2, quarter, hid), BF16),
            pltpu.VMEM((2, quarter, hid), BF16),
            pltpu.VMEM((2, depth, quarter // depth, hid), BF16),
            pltpu.VMEM((2, depth - 1, quarter // depth, hid), BF16),
            pltpu.VMEM((2, 2, 2, depth, quarter // depth, hid), BF16),
            pltpu.VMEM((3, 8, hid), F32),
            pltpu.VMEM((1 + depth, 8, hid), F32),
            dma((2, 2 * depth + 2)),
            dma((2, 2 * depth + 2)),
            dma((1 + depth,)),
            dma((1 + depth,)),
        ]
    act, gfeat, gself, gneigh, gbias = pl.pallas_call(
        functools.partial(kernel, n_row, reduce_here),
        out_shape=(
            jax.ShapeDtypeStruct(block, BF16),
            jax.ShapeDtypeStruct((nodes, f_in), BF16),
            jax.ShapeDtypeStruct((f_in, hid), F32),
            jax.ShapeDtypeStruct((f_in, hid), F32),
            jax.ShapeDtypeStruct((1, hid), F32),
        ),
        in_specs=[vmem, vmem, smem, smem, vmem, vmem, vmem, vmem, vmem],
        out_specs=(vmem,) * 5,
        scratch_shapes=scratch,
        compiler_params=pltpu.CompilerParams(
            collective_id=0, has_side_effects=True, vmem_limit_bytes=60 * 1024 * 1024
        ),
    )(
        features,
        degree.reshape(nodes, 1),
        block_list,
        block_count,
        tiles,
        self_weight,
        neigh_weight,
        bias.reshape(1, hid),
        cotangent,
    )
    gbias = gbias.reshape(hid)
    if not reduce_here:
        gself, gneigh, gbias = lax.psum((gself, gneigh, gbias), "row")
    return act, gfeat, gself, gneigh, gbias


def solution(mesh):
    return jax.shard_map(
        on_device,
        mesh=mesh,
        in_specs=(
            P(("grp", "row"), None),
            P(("grp", "row")),
            P(("grp", "row"), None),
            P(("grp", "row")),
            P(("grp", "row"), None, None),
            P(),
            P(),
            P(),
            P(("grp", "row"), None),
        ),
        out_specs=(
            P(("grp", "row"), None),
            P(("grp", "row"), None),
            P("grp", None),
            P("grp", None),
            P("grp"),
        ),
        check_vma=False,
    )
```

```python
import functools

import jax
import jax.numpy as jnp
from jax import lax
from jax.experimental import pallas as pl
from jax.experimental.pallas import tpu as pltpu
from jax.sharding import PartitionSpec as P

MESH = pl.DeviceIdType.MESH
F32 = jnp.float32
BF16 = jnp.bfloat16
CHUNKS = 4
NEAR = 9
TANH_SCALE = 0.7978845608028654
TANH_CUBE = 0.044715


def dot(a, b):
    return jnp.dot(a, b, preferred_element_type=F32)


def dot_nt(a, b):
    return lax.dot_general(a, b, (((1,), (1,)), ((), ())), preferred_element_type=F32)


def kernel(
    n_row,
    reduce_here,
    feat,
    degree,
    blist,
    bcount,
    tiles,
    w_self,
    w_neigh,
    bias,
    cot,
    act_out,
    gfeat_out,
    gself_out,
    gneigh_out,
    gbias_out,
    win,
    dense,
    dense_t,
    feat_t,
    acc,
    gpre_b,
    msg,
    lane_out,
    lane_in,
    net_out,
    net_in,
    gloc,
    tab,
    fsend,
    frecv,
    lsend,
    lrecv,
    nsend,
    nrecv,
    *red
):
    row = lax.axis_index("row")
    core = lax.rem(row, 2)
    chip = row // 2
    chips = n_row // 2
    side = lax.rem(chip, 2)
    sgn = 2 * side - 1

    def at(chip_off, c):
        return lax.rem(chip + chip_off + 4 * chips, chips) * 2 + c

    other = 1 - core
    partner = at(0, other)
    ypair = at(-sgn, core)
    zpos = at(2 * sgn, core)
    zneg = at(-2 * sgn, core)
    greet = [partner, ypair, zpos, zneg]
    if reduce_here:
        zline = [at(2 * j, core) for j in range(1, chips // 2)]
        greet = [partner, ypair] + zline

    def rc(src, dst, ssem, rsem, dev):
        return pltpu.make_async_remote_copy(
            src_ref=src,
            dst_ref=dst,
            send_sem=ssem,
            recv_sem=rsem,
            device_id={"row": dev},
            device_id_type=MESH,
        )

    barrier = pltpu.get_barrier_semaphore()
    for dev in greet:
        pl.semaphore_signal(barrier, inc=1, device_id={"row": dev}, device_id_type=MESH)
    pl.semaphore_wait(barrier, len(greet))

    nodes = feat.shape[0]
    tile = tiles.shape[1]
    step = nodes // CHUNKS

    def rows_of(ch):
        return pl.ds(pl.multiple_of(ch * step, step), step)

    def loop(count, body):
        def run(i, carry):
            body(i)
            return carry

        lax.fori_loop(0, count, run, 0)

    far = 3 + lax.rem(core + side, 2)
    own_sends = ((0, 3, zpos), (1, 4, zneg), (2, 2, ypair), (3, 1, partner))

    def fcopy(i, src, dst, ch, dev):
        rows = rows_of(ch)
        return rc(win.at[src, rows], win.at[dst, rows], fsend.at[i, ch], frecv.at[dst, ch], dev)

    def fwait(slot, ch):
        fcopy(0, slot, slot, ch, partner).wait_recv()

    def project(ch):
        rows = rows_of(ch)
        win[0, rows, :] = dot(feat[rows, :], w_neigh[...]).astype(BF16)
        for i, dst, dev in own_sends:
            fcopy(i, 0, dst, ch, dev).start()

    loop(CHUNKS, project)

    devs = (
        at(0, core),
        at(0, other),
        at(-sgn, core),
        at(-2 * sgn, core),
        at(2 * sgn, core),
        at(-sgn, other),
        at(2 * (2 * core - 1), other),
        at(sgn, core),
        at(sgn, other),
    )
    for b, dev in enumerate(devs):
        tab[b] = dev
    slots = tiles.shape[0]

    def densify(b):
        for t in range(2):
            column = tab[b] * 2 + t

            def seek(j, found):
                return jnp.maximum(found, jnp.where(blist[j, 1] == column, j, 0))

            slot = lax.fori_loop(0, slots, seek, 0)
            target = blist[slot, 0] - 2 * row
            live = slot < bcount[0]
            block = tiles[slot]
            flipped = block.T
            for r in range(2):
                take = jnp.logical_and(live, target == r)
                here = pl.ds(r * tile, tile)
                there = pl.ds(t * tile, tile)
                dense[b, here, there] = jnp.where(take, block, jnp.zeros_like(block))
                dense_t[b, there, here] = jnp.where(take, flipped, jnp.zeros_like(flipped))

    loop(NEAR, densify)

    def self_part(ch):
        rows = rows_of(ch)
        acc[rows, :] = dot(dense[0, rows, :], win[0])

    loop(CHUNKS, self_part)

    def add_block(b):
        def body(ch):
            rows = rows_of(ch)
            acc[rows, :] += dot(dense[b, rows, :], win[b])

        loop(CHUNKS, body)

    def relay(ch):
        fwait(3, ch)
        fcopy(4, 3, 7, ch, ypair).start()
        fwait(2, ch)
        fcopy(5, 2, 5, ch, partner).start()
        fwait(4, ch)
        fcopy(6, far, 6, ch, partner).start()

    loop(CHUNKS, relay)
    feat_t[...] = feat[...].T

    def arrive(b):
        loop(CHUNKS, lambda ch: fwait(b, ch))
        add_block(b)

    arrive(1)
    add_block(2)
    add_block(3)
    add_block(4)
    arrive(5)
    arrive(6)

    def relay_on(ch):
        fwait(7, ch)
        fcopy(7, 7, 8, ch, partner).start()

    loop(CHUNKS, relay_on)
    add_block(7)
    arrive(8)

    bias_rows = 8

    def activate(ch, bias_sum):
        rows = rows_of(ch)
        inverse = 1.0 / degree[rows, :].astype(F32)
        pre = dot(feat[rows, :], w_self[...]) + acc[rows, :] * inverse + bias[...]
        square = pre * pre
        t = jnp.tanh(TANH_SCALE * (pre + TANH_CUBE * (square * pre)))
        half = 0.5 * (1.0 + t)
        act_out[rows, :] = (pre * half).astype(BF16)
        slope = half + (0.5 * TANH_SCALE) * pre * (1.0 - t * t) * (1.0 + (3.0 * TANH_CUBE) * square)
        grad_pre = cot[rows, :].astype(F32) * slope
        gpre_b[rows, :] = grad_pre.astype(BF16)
        msg[rows, :] = (grad_pre * inverse).astype(BF16)
        return bias_sum + jnp.sum(
            grad_pre.reshape(step // bias_rows, bias_rows, grad_pre.shape[1]), axis=0
        )

    bias_sum = lax.fori_loop(0, CHUNKS, activate, jnp.zeros((bias_rows, acc.shape[1]), F32))

    def term(b, rows):
        return dot(dense_t[b, rows, :], msg[...])

    def lcopy(i, ch):
        rows = rows_of(ch)
        return rc(lane_out.at[i, rows], lane_in.at[i, rows], lsend.at[i, ch], lrecv.at[i, ch], partner)

    def ncopy(i, ch, dev):
        rows = rows_of(ch)
        return rc(net_out.at[i, rows], net_in.at[i, rows], nsend.at[i, ch], nrecv.at[i, ch], dev)

    def lane_term(i, b):
        def body(ch):
            rows = rows_of(ch)
            lane_out[i, rows, :] = term(b, rows).astype(BF16)
            lcopy(i, ch).start()

        return body

    loop(CHUNKS, lane_term(0, 8))
    loop(CHUNKS, lane_term(1, 6))

    def send_relay(ch):
        rows = rows_of(ch)
        mine = term(7, rows)
        lcopy(0, ch).wait_recv()
        net_out[0, rows, :] = (mine + lane_in[0, rows, :].astype(F32)).astype(BF16)
        ncopy(0, ch, ypair).start()

    loop(CHUNKS, send_relay)
    far_pos = (core != side).astype(F32)
    far_neg = 1.0 - far_pos

    def send_pos(ch):
        rows = rows_of(ch)
        mine = term(4, rows)
        lcopy(1, ch).wait_recv()
        net_out[1, rows, :] = (mine + far_pos * lane_in[1, rows, :].astype(F32)).astype(BF16)
        ncopy(1, ch, zpos).start()

    loop(CHUNKS, send_pos)
    loop(CHUNKS, lane_term(2, 5))

    def send_y(ch):
        rows = rows_of(ch)
        mine = term(2, rows)
        lcopy(2, ch).wait_recv()
        net_out[2, rows, :] = (mine + lane_in[2, rows, :].astype(F32)).astype(BF16)
        ncopy(2, ch, ypair).start()

    loop(CHUNKS, send_y)

    def send_neg(ch):
        rows = rows_of(ch)
        mine = term(3, rows) + far_neg * lane_in[1, rows, :].astype(F32)
        ncopy(0, ch, ypair).wait_recv()
        net_out[3, rows, :] = (mine + net_in[0, rows, :].astype(F32)).astype(BF16)
        ncopy(3, ch, zneg).start()

    loop(CHUNKS, send_neg)
    loop(CHUNKS, lane_term(3, 1))

    f_in = feat.shape[1]
    half_f, quarter_f = f_in // 2, f_in // 4
    f_step = f_in // CHUNKS

    def weight_grad(g, source):
        def body(i):
            rows = pl.ds(pl.multiple_of(i * f_step, f_step), f_step)
            gloc[g, rows, :] = dot(feat_t[rows, :], source[...])

        loop(CHUNKS, body)

    weight_grad(0, gpre_b)

    if reduce_here:
        (s1, r1, s2, r2, s3, r3, gath, b_out, b_in, gs, gr, bs, br) = red
        depth = chips // 2
        piece_f = quarter_f // depth
        z = chip // 2
        my_half = pl.multiple_of(core * half_f, half_f)
        not_half = pl.multiple_of(other * half_f, half_f)
        my_quarter = pl.multiple_of(my_half + side * quarter_f, quarter_f)
        not_quarter = pl.multiple_of(my_half + (1 - side) * quarter_f, quarter_f)
        my_piece = pl.multiple_of(my_quarter + z * piece_f, piece_f)
        far_z = [lax.rem(z + j, depth) for j in range(1, depth)]

        def c1(g):
            return rc(s1.at[g], r1.at[g], gs.at[g, 0], gr.at[g, 0], partner)

        def c2(g):
            return rc(s2.at[g], r2.at[g], gs.at[g, 1], gr.at[g, 1], ypair)

        def c3(g, j):
            return rc(
                s3.at[g, j], r3.at[g, j], gs.at[g, 2 + j], gr.at[g, 2 + j], zline[j]
            )

        def c4(g, j):
            return rc(
                gath.at[g, 0, 0, 0],
                gath.at[g, 0, 0, j + 1],
                gs.at[g, 1 + depth + j],
                gr.at[g, 1 + depth + j],
                zline[j],
            )

        last = 2 * depth

        def c5(g):
            return rc(gath.at[g, 0, 0], gath.at[g, 0, 1], gs.at[g, last], gr.at[g, last], ypair)

        def c6(g):
            return rc(gath.at[g, 0], gath.at[g, 1], gs.at[g, last + 1], gr.at[g, last + 1], partner)

        def stage1(g):
            for a in range(2):
                start = not_half + (side if a == 0 else 1 - side) * quarter_f
                rows = pl.ds(pl.multiple_of(start, quarter_f), quarter_f)
                s1[g, a] = gloc[g, rows, :].astype(BF16)
            c1(g).start()

        def stage2(g):
            c1(g).wait_recv()
            s2[g] = (
                gloc[g, pl.ds(not_quarter, quarter_f), :]
                + r1[g, 1].astype(F32)
            ).astype(BF16)
            c2(g).start()

        def stage3(g):
            mine = (
                gloc[g, pl.ds(my_quarter, quarter_f), :]
                + r1[g, 0].astype(F32)
            )
            c2(g).wait_recv()
            mine = mine + r2[g].astype(F32)
            gloc[g, pl.ds(my_quarter, quarter_f), :] = mine
            for j in range(depth - 1):
                start = pl.multiple_of(my_quarter + far_z[j] * piece_f, piece_f)
                s3[g, j] = gloc[g, pl.ds(start, piece_f), :].astype(BF16)
            for j in range(depth - 1):
                c3(g, j).start()

        def stage4(g):
            total = gloc[g, pl.ds(my_piece, piece_f), :]
            for j in range(depth - 1):
                c3(g, j).wait_recv()
                total = total + r3[g, j].astype(F32)
            gath[g, 0, 0, 0] = total.astype(BF16)
            for j in range(depth - 1):
                c4(g, j).start()

        def stage5(g):
            for j in range(depth - 1):
                c4(g, j).wait_recv()
            c5(g).start()

        def stage6(g):
            c5(g).wait_recv()
            c6(g).start()

        def stage7(g, out):
            c6(g).wait_recv()
            for a in range(2):
                for b in range(2):
                    base = (core if a == 0 else other) * half_f
                    base = base + (side if b == 0 else 1 - side) * quarter_f
                    for j in range(depth):
                        start = base + lax.rem(z + depth - j, depth) * piece_f
                        rows = pl.ds(pl.multiple_of(start, piece_f), piece_f)
                        out[rows, :] = gath[g, a, b, j].astype(F32)

        def bcopy(i, src, dev):
            return rc(b_out.at[src], b_in.at[i], bs.at[i], br.at[i], dev)

        b_out[0] = bias_sum
        bcopy(0, 0, partner).start()
        stage1(0)
        bcopy(0, 0, partner).wait_recv()
        b_out[1] = b_out[0] + b_in[0]
        bcopy(1, 1, ypair).start()
        stage2(0)
        bcopy(1, 1, ypair).wait_recv()
        b_out[2] = b_out[1] + b_in[1]
        for j in range(depth - 1):
            bcopy(2 + j, 2, zline[j]).start()

    g_rows = nodes // CHUNKS

    def feature_grad(ch):
        rows = rows_of(ch)
        gfeat_out[rows, :] = dot_nt(gpre_b[rows, :], w_self[...]).astype(BF16)

    def gather_own(ch):
        rows = rows_of(ch)
        total = term(0, rows)
        lcopy(3, ch).wait_recv()
        total = total + lane_in[3, rows, :].astype(F32)
        ncopy(2, ch, ypair).wait_recv()
        total = total + net_in[2, rows, :].astype(F32)
        ncopy(1, ch, zpos).wait_recv()
        total = total + net_in[1, rows, :].astype(F32)
        ncopy(3, ch, zneg).wait_recv()
        total = total + net_in[3, rows, :].astype(F32)
        msg_back[rows, :] = total.astype(BF16)

    msg_back = win.at[0]
    if reduce_here:
        stage3(0)
        stage4(0)
    for i, src, dst in ((0, 0, 3), (1, 0, 4), (2, 0, 2), (3, 0, 1), (4, 3, 7), (5, 2, 5), (6, 3, 6), (7, 7, 8)):
        loop(CHUNKS, lambda ch, i=i, src=src, dst=dst: fcopy(i, src, dst, ch, partner).wait_send())
    loop(CHUNKS, gather_own)
    weight_grad(1, msg_back)
    if reduce_here:
        stage1(1)
        stage5(0)
        stage2(1)
        stage6(0)
        stage3(1)

    def feature_grad(ch):
        rows = rows_of(ch)
        gfeat_out[rows, :] = (
            dot_nt(gpre_b[rows, :], w_self[...]) + dot_nt(msg_back[rows, :], w_neigh[...])
        ).astype(BF16)

    loop(CHUNKS, feature_grad)
    if reduce_here:
        stage4(1)
        stage7(0, gself_out)
        total = b_out[2]
        for j in range(depth - 1):
            bcopy(2 + j, 2, zline[j]).wait_recv()
            total = total + b_in[2 + j]
        gbias_out[...] = jnp.sum(total, axis=0, keepdims=True)
        stage5(1)
        stage6(1)
        stage7(1, gneigh_out)
        for g in range(2):
            c1(g).wait_send()
            c2(g).wait_send()
            for j in range(depth - 1):
                c3(g, j).wait_send()
                c4(g, j).wait_send()
            c5(g).wait_send()
            c6(g).wait_send()
        bcopy(0, 0, partner).wait_send()
        bcopy(1, 1, ypair).wait_send()
        for j in range(depth - 1):
            bcopy(2 + j, 2, zline[j]).wait_send()
    else:
        gself_out[...] = gloc[0]
        gneigh_out[...] = gloc[1]
        gbias_out[...] = jnp.sum(bias_sum, axis=0, keepdims=True)

    def drain(ch):
        for i in range(4):
            lcopy(i, ch).wait_send()
        for i, dev in enumerate((ypair, zpos, ypair, zneg)):
            ncopy(i, ch, dev).wait_send()

    loop(CHUNKS, drain)


def on_device(
    features, degree, block_list, block_count, tiles, self_weight, neigh_weight, bias, cotangent
):
    nodes, f_in = features.shape
    hid = neigh_weight.shape[1]
    n_row = lax.axis_size("row")
    depth = n_row // 4
    reduce_here = f_in % (4 * depth * 16) == 0 and depth >= 3 and depth <= 4
    vmem = pl.BlockSpec(memory_space=pltpu.VMEM)
    smem = pl.BlockSpec(memory_space=pltpu.SMEM)
    dma = pltpu.SemaphoreType.DMA
    block = (nodes, hid)
    scratch = [
        pltpu.VMEM((NEAR,) + block, BF16),
        pltpu.VMEM((NEAR, nodes, nodes), BF16),
        pltpu.VMEM((NEAR, nodes, nodes), BF16),
        pltpu.VMEM((f_in, nodes), BF16),
        pltpu.VMEM(block, F32),
        pltpu.VMEM(block, BF16),
        pltpu.VMEM(block, BF16),
        pltpu.VMEM((4,) + block, BF16),
        pltpu.VMEM((4,) + block, BF16),
        pltpu.VMEM((4,) + block, BF16),
        pltpu.VMEM((4,) + block, BF16),
        pltpu.VMEM((2, f_in, hid), F32),
        pltpu.SMEM((NEAR,), jnp.int32),
        dma((8, CHUNKS)),
        dma((NEAR, CHUNKS)),
        dma((4, CHUNKS)),
        dma((4, CHUNKS)),
        dma((4, CHUNKS)),
        dma((4, CHUNKS)),
    ]
    if reduce_here:
        quarter = f_in // 4
        scratch += [
            pltpu.VMEM((2, 2, quarter, hid), BF16),
            pltpu.VMEM((2, 2, quarter, hid), BF16),
            pltpu.VMEM((2, quarter, hid), BF16),
            pltpu.VMEM((2, quarter, hid), BF16),
            pltpu.VMEM((2, depth - 1, quarter // depth, hid), BF16),
            pltpu.VMEM((2, depth - 1, quarter // depth, hid), BF16),
            pltpu.VMEM((2, 2, 2, depth, quarter // depth, hid), BF16),
            pltpu.VMEM((3, 8, hid), F32),
            pltpu.VMEM((1 + depth, 8, hid), F32),
            dma((2, 2 * depth + 2)),
            dma((2, 2 * depth + 2)),
            dma((1 + depth,)),
            dma((1 + depth,)),
        ]
    act, gfeat, gself, gneigh, gbias = pl.pallas_call(
        functools.partial(kernel, n_row, reduce_here),
        out_shape=(
            jax.ShapeDtypeStruct(block, BF16),
            jax.ShapeDtypeStruct((nodes, f_in), BF16),
            jax.ShapeDtypeStruct((f_in, hid), F32),
            jax.ShapeDtypeStruct((f_in, hid), F32),
            jax.ShapeDtypeStruct((1, hid), F32),
        ),
        in_specs=[vmem, vmem, smem, smem, vmem, vmem, vmem, vmem, vmem],
        out_specs=(vmem,) * 5,
        scratch_shapes=scratch,
        compiler_params=pltpu.CompilerParams(
            collective_id=0, has_side_effects=True, vmem_limit_bytes=60 * 1024 * 1024
        ),
    )(
        features,
        degree.reshape(nodes, 1),
        block_list,
        block_count,
        tiles,
        self_weight,
        neigh_weight,
        bias.reshape(1, hid),
        cotangent,
    )
    gbias = gbias.reshape(hid)
    if not reduce_here:
        gself, gneigh, gbias = lax.psum((gself, gneigh, gbias), "row")
    return act, gfeat, gself, gneigh, gbias


def solution(mesh):
    return jax.shard_map(
        on_device,
        mesh=mesh,
        in_specs=(
            P(("grp", "row"), None),
            P(("grp", "row")),
            P(("grp", "row"), None),
            P(("grp", "row")),
            P(("grp", "row"), None, None),
            P(),
            P(),
            P(),
            P(("grp", "row"), None),
        ),
        out_specs=(
            P(("grp", "row"), None),
            P(("grp", "row"), None),
            P("grp", None),
            P("grp", None),
            P("grp"),
        ),
        check_vma=False,
    )
```

```python
import functools

import jax
import jax.numpy as jnp
from jax import lax
from jax.experimental import pallas as pl
from jax.experimental.pallas import tpu as pltpu
from jax.sharding import PartitionSpec as P

MESH = pl.DeviceIdType.MESH
F32 = jnp.float32
BF16 = jnp.bfloat16
CHUNKS = 4
NEAR = 9
TANH_SCALE = 0.7978845608028654
TANH_CUBE = 0.044715


def dot(a, b):
    return jnp.dot(a, b, preferred_element_type=F32)


def dot_nt(a, b):
    return lax.dot_general(a, b, (((1,), (1,)), ((), ())), preferred_element_type=F32)


def kernel(
    n_row,
    reduce_here,
    feat,
    degree,
    blist,
    bcount,
    tiles,
    w_self,
    w_neigh,
    bias,
    cot,
    act_out,
    gfeat_out,
    gself_out,
    gneigh_out,
    gbias_out,
    win,
    dense,
    dense_t,
    feat_t,
    acc,
    gpre_b,
    msg,
    lane_out,
    lane_in,
    net_out,
    net_in,
    gloc,
    tab,
    fsend,
    frecv,
    lsend,
    lrecv,
    nsend,
    nrecv,
    *red
):
    row = lax.axis_index("row")
    core = lax.rem(row, 2)
    chip = row // 2
    chips = n_row // 2
    side = lax.rem(chip, 2)
    sgn = 2 * side - 1

    def at(chip_off, c):
        return lax.rem(chip + chip_off + 4 * chips, chips) * 2 + c

    other = 1 - core
    partner = at(0, other)
    ypair = at(-sgn, core)
    zpos = at(2 * sgn, core)
    zneg = at(-2 * sgn, core)
    greet = [partner, ypair, zpos, zneg]
    if reduce_here:
        zline = [at(2 * j, core) for j in range(1, chips // 2)]
        greet = [partner, ypair] + zline

    def rc(src, dst, ssem, rsem, dev):
        return pltpu.make_async_remote_copy(
            src_ref=src,
            dst_ref=dst,
            send_sem=ssem,
            recv_sem=rsem,
            device_id={"row": dev},
            device_id_type=MESH,
        )

    barrier = pltpu.get_barrier_semaphore()
    for dev in greet:
        pl.semaphore_signal(barrier, inc=1, device_id={"row": dev}, device_id_type=MESH)
    pl.semaphore_wait(barrier, len(greet))

    nodes = feat.shape[0]
    tile = tiles.shape[1]
    step = nodes // CHUNKS

    def rows_of(ch):
        return pl.ds(pl.multiple_of(ch * step, step), step)

    def loop(count, body):
        def run(i, carry):
            body(i)
            return carry

        lax.fori_loop(0, count, run, 0)

    far = 3 + lax.rem(core + side, 2)
    own_sends = ((0, 3, zpos), (1, 4, zneg), (2, 2, ypair), (3, 1, partner))

    def fcopy(i, src, dst, ch, dev):
        rows = rows_of(ch)
        return rc(win.at[src, rows], win.at[dst, rows], fsend.at[i, ch], frecv.at[dst, ch], dev)

    def fwait(slot, ch):
        fcopy(0, slot, slot, ch, partner).wait_recv()

    def project(ch):
        rows = rows_of(ch)
        win[0, rows, :] = dot(feat[rows, :], w_neigh[...]).astype(BF16)
        for i, dst, dev in own_sends:
            fcopy(i, 0, dst, ch, dev).start()

    loop(CHUNKS, project)

    devs = (
        at(0, core),
        at(0, other),
        at(-sgn, core),
        at(-2 * sgn, core),
        at(2 * sgn, core),
        at(-sgn, other),
        at(2 * (2 * core - 1), other),
        at(sgn, core),
        at(sgn, other),
    )
    for b, dev in enumerate(devs):
        tab[b] = dev
    slots = tiles.shape[0]

    def densify(b):
        for t in range(2):
            column = tab[b] * 2 + t

            def seek(j, found):
                return jnp.maximum(found, jnp.where(blist[j, 1] == column, j, 0))

            slot = lax.fori_loop(0, slots, seek, 0)
            target = blist[slot, 0] - 2 * row
            live = slot < bcount[0]
            block = tiles[slot]
            flipped = block.T
            for r in range(2):
                take = jnp.logical_and(live, target == r)
                here = pl.ds(r * tile, tile)
                there = pl.ds(t * tile, tile)
                dense[b, here, there] = jnp.where(take, block, jnp.zeros_like(block))
                dense_t[b, there, here] = jnp.where(take, flipped, jnp.zeros_like(flipped))

    def add_block(b):
        def body(ch):
            rows = rows_of(ch)
            acc[rows, :] += dot(dense[b, rows, :], win[b])

        loop(CHUNKS, body)

    def relay(ch):
        fwait(3, ch)
        fcopy(4, 3, 7, ch, ypair).start()
        fwait(2, ch)
        fcopy(5, 2, 5, ch, partner).start()
        fwait(4, ch)
        fcopy(6, far, 6, ch, partner).start()

    def densify_and_relay(ch):
        densify(2 * ch)
        densify(2 * ch + 1)
        relay(ch)

    loop(CHUNKS, densify_and_relay)
    densify(NEAR - 1)

    def self_part(ch):
        rows = rows_of(ch)
        acc[rows, :] = dot(dense[0, rows, :], win[0])

    loop(CHUNKS, self_part)

    feat_t[...] = feat[...].T

    def arrive(b):
        loop(CHUNKS, lambda ch: fwait(b, ch))
        add_block(b)

    arrive(1)
    add_block(2)
    add_block(3)
    add_block(4)
    arrive(5)
    arrive(6)

    def relay_on(ch):
        fwait(7, ch)
        fcopy(7, 7, 8, ch, partner).start()

    loop(CHUNKS, relay_on)
    add_block(7)
    arrive(8)

    bias_rows = 8

    def activate(ch, bias_sum):
        rows = rows_of(ch)
        per_node = 1.0 / degree[pl.ds(ch, 1), :].astype(F32)
        inverse = jnp.broadcast_to(per_node, (step, step)).T[:, :1]
        pre = dot(feat[rows, :], w_self[...]) + acc[rows, :] * inverse + bias[...]
        square = pre * pre
        t = jnp.tanh(TANH_SCALE * (pre + TANH_CUBE * (square * pre)))
        half = 0.5 * (1.0 + t)
        act_out[rows, :] = (pre * half).astype(BF16)
        slope = half + (0.5 * TANH_SCALE) * pre * (1.0 - t * t) * (1.0 + (3.0 * TANH_CUBE) * square)
        grad_pre = cot[rows, :].astype(F32) * slope
        gpre_b[rows, :] = grad_pre.astype(BF16)
        msg[rows, :] = (grad_pre * inverse).astype(BF16)
        return bias_sum + jnp.sum(
            grad_pre.reshape(step // bias_rows, bias_rows, grad_pre.shape[1]), axis=0
        )

    bias_sum = lax.fori_loop(0, CHUNKS, activate, jnp.zeros((bias_rows, acc.shape[1]), F32))

    def term(b, rows):
        return dot(dense_t[b, rows, :], msg[...])

    def lcopy(i, ch):
        rows = rows_of(ch)
        return rc(lane_out.at[i, rows], lane_in.at[i, rows], lsend.at[i, ch], lrecv.at[i, ch], partner)

    def ncopy(i, ch, dev):
        rows = rows_of(ch)
        return rc(net_out.at[i, rows], net_in.at[i, rows], nsend.at[i, ch], nrecv.at[i, ch], dev)

    def lane_term(i, b):
        def body(ch):
            rows = rows_of(ch)
            lane_out[i, rows, :] = term(b, rows).astype(BF16)
            lcopy(i, ch).start()

        return body

    loop(CHUNKS, lane_term(0, 8))
    loop(CHUNKS, lane_term(1, 6))

    def send_relay(ch):
        rows = rows_of(ch)
        mine = term(7, rows)
        lcopy(0, ch).wait_recv()
        net_out[0, rows, :] = (mine + lane_in[0, rows, :].astype(F32)).astype(BF16)
        ncopy(0, ch, ypair).start()

    loop(CHUNKS, send_relay)
    far_pos = (core != side).astype(F32)
    far_neg = 1.0 - far_pos

    def send_pos(ch):
        rows = rows_of(ch)
        mine = term(4, rows)
        lcopy(1, ch).wait_recv()
        net_out[1, rows, :] = (mine + far_pos * lane_in[1, rows, :].astype(F32)).astype(BF16)
        ncopy(1, ch, zpos).start()

    loop(CHUNKS, send_pos)
    loop(CHUNKS, lane_term(2, 5))

    def send_y(ch):
        rows = rows_of(ch)
        mine = term(2, rows)
        lcopy(2, ch).wait_recv()
        net_out[2, rows, :] = (mine + lane_in[2, rows, :].astype(F32)).astype(BF16)
        ncopy(2, ch, ypair).start()

    loop(CHUNKS, send_y)

    def send_neg(ch):
        rows = rows_of(ch)
        mine = term(3, rows) + far_neg * lane_in[1, rows, :].astype(F32)
        ncopy(0, ch, ypair).wait_recv()
        net_out[3, rows, :] = (mine + net_in[0, rows, :].astype(F32)).astype(BF16)
        ncopy(3, ch, zneg).start()

    loop(CHUNKS, send_neg)
    loop(CHUNKS, lane_term(3, 1))

    f_in = feat.shape[1]
    half_f, quarter_f = f_in // 2, f_in // 4
    f_step = f_in // CHUNKS

    width = gloc.shape[2]

    def reduce_stages():
        (s1, r1, s2, r2, s3, r3, gath, b_out, b_in, gs, gr, bs, br) = red
        depth = chips // 2
        piece_f = quarter_f // depth
        z = chip // 2
        my_half = pl.multiple_of(core * half_f, half_f)
        not_half = pl.multiple_of(other * half_f, half_f)
        my_quarter = pl.multiple_of(my_half + side * quarter_f, quarter_f)
        not_quarter = pl.multiple_of(my_half + (1 - side) * quarter_f, quarter_f)
        my_piece = pl.multiple_of(my_quarter + z * piece_f, piece_f)
        far_z = [lax.rem(z + j, depth) for j in range(1, depth)]

        def c1(g):
            return rc(s1.at[g], r1.at[g], gs.at[g, 0], gr.at[g, 0], partner)

        def c2(g):
            return rc(s2.at[g], r2.at[g], gs.at[g, 1], gr.at[g, 1], ypair)

        def c3(g, j):
            return rc(
                s3.at[g, j], r3.at[g, j], gs.at[g, 2 + j], gr.at[g, 2 + j], zline[j]
            )

        def c4(g, j):
            return rc(
                gath.at[g, 0, 0, 0],
                gath.at[g, 0, 0, j + 1],
                gs.at[g, 1 + depth + j],
                gr.at[g, 1 + depth + j],
                zline[j],
            )

        last = 2 * depth

        def c5(g):
            return rc(gath.at[g, 0, 0], gath.at[g, 0, 1], gs.at[g, last], gr.at[g, last], ypair)

        def c6(g):
            return rc(gath.at[g, 0], gath.at[g, 1], gs.at[g, last + 1], gr.at[g, last + 1], partner)

        def stage1(g):
            for a in range(2):
                start = not_half + (side if a == 0 else 1 - side) * quarter_f
                rows = pl.ds(pl.multiple_of(start, quarter_f), quarter_f)
                s1[g, a] = gloc[g, rows, :].astype(BF16)
            c1(g).start()

        def stage2(g):
            c1(g).wait_recv()
            s2[g] = (
                gloc[g, pl.ds(not_quarter, quarter_f), :]
                + r1[g, 1].astype(F32)
            ).astype(BF16)
            c2(g).start()

        def stage3(g):
            mine = (
                gloc[g, pl.ds(my_quarter, quarter_f), :]
                + r1[g, 0].astype(F32)
            )
            c2(g).wait_recv()
            mine = mine + r2[g].astype(F32)
            gloc[g, pl.ds(my_quarter, quarter_f), :] = mine
            for j in range(depth - 1):
                start = pl.multiple_of(my_quarter + far_z[j] * piece_f, piece_f)
                s3[g, j] = gloc[g, pl.ds(start, piece_f), :].astype(BF16)
            for j in range(depth - 1):
                c3(g, j).start()

        def stage4(g):
            total = gloc[g, pl.ds(my_piece, piece_f), :]
            for j in range(depth - 1):
                c3(g, j).wait_recv()
                total = total + r3[g, j].astype(F32)
            gath[g, 0, 0, 0] = total.astype(BF16)
            for j in range(depth - 1):
                c4(g, j).start()

        def stage5(g):
            for j in range(depth - 1):
                c4(g, j).wait_recv()
            c5(g).start()

        def stage6(g):
            c5(g).wait_recv()
            c6(g).start()

        def stage7(g):
            out = gself_out if g < 2 else gneigh_out
            cols = pl.ds(g % 2 * width, width)
            c6(g).wait_recv()
            for a in range(2):
                for b in range(2):
                    base = (core if a == 0 else other) * half_f
                    base = base + (side if b == 0 else 1 - side) * quarter_f
                    for j in range(depth):
                        start = base + lax.rem(z + depth - j, depth) * piece_f
                        rows = pl.ds(pl.multiple_of(start, piece_f), piece_f)
                        out[rows, cols] = gath[g, a, b, j]

        def bcopy(i, src, dev):
            return rc(b_out.at[src], b_in.at[i], bs.at[i], br.at[i], dev)

        def bias_start():
            b_out[0] = bias_sum
            bcopy(0, 0, partner).start()
            bcopy(0, 0, partner).wait_recv()
            b_out[1] = b_out[0] + b_in[0]
            bcopy(1, 1, ypair).start()
            bcopy(1, 1, ypair).wait_recv()
            b_out[2] = b_out[1] + b_in[1]
            for j in range(depth - 1):
                bcopy(2 + j, 2, zline[j]).start()

        def bias_end():
            total = b_out[2]
            for j in range(depth - 1):
                bcopy(2 + j, 2, zline[j]).wait_recv()
                total = total + b_in[2 + j]
            gbias_out[...] = jnp.sum(total, axis=0, keepdims=True)

        def settle():
            for g in range(4):
                c1(g).wait_send()
                c2(g).wait_send()
                for j in range(depth - 1):
                    c3(g, j).wait_send()
                    c4(g, j).wait_send()
                c5(g).wait_send()
                c6(g).wait_send()
            bcopy(0, 0, partner).wait_send()
            bcopy(1, 1, ypair).wait_send()
            for j in range(depth - 1):
                bcopy(2 + j, 2, zline[j]).wait_send()

        return (
            stage1, stage2, stage3, stage4, stage5, stage6, stage7, bias_start, bias_end, settle
        )

    def weight_grad(u, source):
        cols = pl.ds(u % 2 * width, width)

        def body(i):
            rows = pl.ds(pl.multiple_of(i * f_step, f_step), f_step)
            gloc[u, rows, :] = dot(feat_t[rows, :], source[:, cols])

        loop(CHUNKS, body)

    weight_grad(0, gpre_b)
    if reduce_here:
        stages = reduce_stages()
        stage1, stage2, stage3, stage4, stage5, stage6, stage7, bias_start, bias_end, settle = stages
        stage1(0)
    weight_grad(1, gpre_b)
    if reduce_here:
        stage1(1)
        bias_start()
        stage2(0)
        stage2(1)

    def gather_own(ch):
        rows = rows_of(ch)
        total = term(0, rows)
        lcopy(3, ch).wait_recv()
        total = total + lane_in[3, rows, :].astype(F32)
        ncopy(2, ch, ypair).wait_recv()
        total = total + net_in[2, rows, :].astype(F32)
        ncopy(1, ch, zpos).wait_recv()
        total = total + net_in[1, rows, :].astype(F32)
        ncopy(3, ch, zneg).wait_recv()
        total = total + net_in[3, rows, :].astype(F32)
        msg_back[rows, :] = total.astype(BF16)

    msg_back = win.at[0]
    if reduce_here:
        stage3(0)
        stage3(1)
    for i, src, dst in ((0, 0, 3), (1, 0, 4), (2, 0, 2), (3, 0, 1), (4, 3, 7), (5, 2, 5), (6, 3, 6), (7, 7, 8)):
        loop(CHUNKS, lambda ch, i=i, src=src, dst=dst: fcopy(i, src, dst, ch, partner).wait_send())
    loop(CHUNKS, gather_own)

    def feature_grad(ch):
        rows = rows_of(ch)
        gfeat_out[rows, :] = (
            dot_nt(gpre_b[rows, :], w_self[...]) + dot_nt(msg_back[rows, :], w_neigh[...])
        ).astype(BF16)

    weight_grad(2, msg_back)
    if reduce_here:
        stage1(2)
    weight_grad(3, msg_back)
    if reduce_here:
        stage1(3)
        stage2(2)
        stage4(0)
        stage2(3)
        stage4(1)
        stage3(2)
        stage5(0)
        stage3(3)
        stage5(1)
        stage6(0)
        stage4(2)
        stage6(1)
        stage4(3)
        stage5(2)
        stage5(3)
    loop(CHUNKS, feature_grad)
    if reduce_here:
        stage6(2)
        stage6(3)
        stage7(0)
        stage7(1)
        bias_end()
        stage7(2)
        stage7(3)
        settle()
    else:
        for u in range(4):
            cols = pl.ds(u % 2 * width, width)
            out = gself_out if u < 2 else gneigh_out
            out[:, cols] = gloc[u]
        gbias_out[...] = jnp.sum(bias_sum, axis=0, keepdims=True)

    def drain(ch):
        for i in range(4):
            lcopy(i, ch).wait_send()
        for i, dev in enumerate((ypair, zpos, ypair, zneg)):
            ncopy(i, ch, dev).wait_send()

    loop(CHUNKS, drain)


def on_device(
    features, degree, block_list, block_count, tiles, self_weight, neigh_weight, bias, cotangent
):
    nodes, f_in = features.shape
    hid = neigh_weight.shape[1]
    n_row = lax.axis_size("row")
    depth = n_row // 4
    reduce_here = f_in % (4 * depth * 16) == 0 and depth >= 3 and depth <= 4
    vmem = pl.BlockSpec(memory_space=pltpu.VMEM)
    smem = pl.BlockSpec(memory_space=pltpu.SMEM)
    dma = pltpu.SemaphoreType.DMA
    block = (nodes, hid)
    scratch = [
        pltpu.VMEM((NEAR,) + block, BF16),
        pltpu.VMEM((NEAR, nodes, nodes), BF16),
        pltpu.VMEM((NEAR, nodes, nodes), BF16),
        pltpu.VMEM((f_in, nodes), BF16),
        pltpu.VMEM(block, F32),
        pltpu.VMEM(block, BF16),
        pltpu.VMEM(block, BF16),
        pltpu.VMEM((4,) + block, BF16),
        pltpu.VMEM((4,) + block, BF16),
        pltpu.VMEM((4,) + block, BF16),
        pltpu.VMEM((4,) + block, BF16),
        pltpu.VMEM((4, f_in, hid // 2), F32),
        pltpu.SMEM((NEAR,), jnp.int32),
        dma((8, CHUNKS)),
        dma((NEAR, CHUNKS)),
        dma((4, CHUNKS)),
        dma((4, CHUNKS)),
        dma((4, CHUNKS)),
        dma((4, CHUNKS)),
    ]
    if reduce_here:
        quarter, wide = f_in // 4, hid // 2
        scratch += [
            pltpu.VMEM((4, 2, quarter, wide), BF16),
            pltpu.VMEM((4, 2, quarter, wide), BF16),
            pltpu.VMEM((4, quarter, wide), BF16),
            pltpu.VMEM((4, quarter, wide), BF16),
            pltpu.VMEM((4, depth - 1, quarter // depth, wide), BF16),
            pltpu.VMEM((4, depth - 1, quarter // depth, wide), BF16),
            pltpu.VMEM((4, 2, 2, depth, quarter // depth, wide), BF16),
            pltpu.VMEM((3, 8, hid), F32),
            pltpu.VMEM((1 + depth, 8, hid), F32),
            dma((4, 2 * depth + 2)),
            dma((4, 2 * depth + 2)),
            dma((1 + depth,)),
            dma((1 + depth,)),
        ]
    act, gfeat, gself, gneigh, gbias = pl.pallas_call(
        functools.partial(kernel, n_row, reduce_here),
        out_shape=(
            jax.ShapeDtypeStruct(block, BF16),
            jax.ShapeDtypeStruct((nodes, f_in), BF16),
            jax.ShapeDtypeStruct((f_in, hid), BF16 if reduce_here else F32),
            jax.ShapeDtypeStruct((f_in, hid), BF16 if reduce_here else F32),
            jax.ShapeDtypeStruct((1, hid), F32),
        ),
        in_specs=[vmem, vmem, smem, smem, vmem, vmem, vmem, vmem, vmem],
        out_specs=(vmem,) * 5,
        scratch_shapes=scratch,
        compiler_params=pltpu.CompilerParams(
            collective_id=0, has_side_effects=True, vmem_limit_bytes=60 * 1024 * 1024
        ),
    )(
        features,
        degree.reshape(CHUNKS, nodes // CHUNKS),
        block_list,
        block_count,
        tiles,
        self_weight,
        neigh_weight,
        bias.reshape(1, hid),
        cotangent,
    )
    gbias = gbias.reshape(hid)
    gself, gneigh = gself.astype(F32), gneigh.astype(F32)
    if not reduce_here:
        gself, gneigh, gbias = lax.psum((gself, gneigh, gbias), "row")
    return act, gfeat, gself, gneigh, gbias


def solution(mesh):
    return jax.shard_map(
        on_device,
        mesh=mesh,
        in_specs=(
            P(("grp", "row"), None),
            P(("grp", "row")),
            P(("grp", "row"), None),
            P(("grp", "row")),
            P(("grp", "row"), None, None),
            P(),
            P(),
            P(),
            P(("grp", "row"), None),
        ),
        out_specs=(
            P(("grp", "row"), None),
            P(("grp", "row"), None),
            P("grp", None),
            P("grp", None),
            P("grp"),
        ),
        check_vma=False,
    )
```

```python
import functools

import jax
import jax.numpy as jnp
from jax import lax
from jax.experimental import pallas as pl
from jax.experimental.pallas import tpu as pltpu
from jax.sharding import PartitionSpec as P

MESH = pl.DeviceIdType.MESH
F32 = jnp.float32
BF16 = jnp.bfloat16
CHUNKS = 2
NEAR = 9
TANH_SCALE = 0.7978845608028654
TANH_CUBE = 0.044715


def dot(a, b):
    return jnp.dot(a, b, preferred_element_type=F32)


def dot_nt(a, b):
    return lax.dot_general(a, b, (((1,), (1,)), ((), ())), preferred_element_type=F32)


def kernel(
    n_row,
    reduce_here,
    feat,
    degree,
    blist,
    bcount,
    tiles,
    w_self,
    w_neigh,
    bias,
    cot,
    act_out,
    gfeat_out,
    gself_out,
    gneigh_out,
    gbias_out,
    win,
    dense,
    dense_t,
    feat_t,
    acc,
    gpre_b,
    msg,
    lane_out,
    lane_in,
    net_out,
    net_in,
    gloc,
    tab,
    fsend,
    frecv,
    lsend,
    lrecv,
    nsend,
    nrecv,
    *red
):
    row = lax.axis_index("row")
    core = lax.rem(row, 2)
    chip = row // 2
    chips = n_row // 2
    side = lax.rem(chip, 2)
    sgn = 2 * side - 1

    def at(chip_off, c):
        return lax.rem(chip + chip_off + 4 * chips, chips) * 2 + c

    other = 1 - core
    partner = at(0, other)
    ypair = at(-sgn, core)
    zpos = at(2 * sgn, core)
    zneg = at(-2 * sgn, core)
    greet = [partner, ypair, zpos, zneg]
    if reduce_here:
        zline = [at(2 * j, core) for j in range(1, chips // 2)]
        greet = [partner, ypair] + zline

    def rc(src, dst, ssem, rsem, dev):
        return pltpu.make_async_remote_copy(
            src_ref=src,
            dst_ref=dst,
            send_sem=ssem,
            recv_sem=rsem,
            device_id={"row": dev},
            device_id_type=MESH,
        )

    barrier = pltpu.get_barrier_semaphore()
    for dev in greet:
        pl.semaphore_signal(barrier, inc=1, device_id={"row": dev}, device_id_type=MESH)
    pl.semaphore_wait(barrier, len(greet))

    nodes = feat.shape[0]
    tile = tiles.shape[1]
    step = nodes // CHUNKS

    def rows_of(ch):
        return pl.ds(pl.multiple_of(ch * step, step), step)

    def loop(count, body):
        def run(i, carry):
            body(i)
            return carry

        lax.fori_loop(0, count, run, 0)

    far = 3 + lax.rem(core + side, 2)
    own_sends = ((0, 3, zpos), (1, 4, zneg), (2, 2, ypair), (3, 1, partner))

    def fcopy(i, src, dst, ch, dev):
        rows = rows_of(ch)
        return rc(win.at[src, rows], win.at[dst, rows], fsend.at[i, ch], frecv.at[dst, ch], dev)

    def fwait(slot, ch):
        fcopy(0, slot, slot, ch, partner).wait_recv()

    def project(ch):
        rows = rows_of(ch)
        win[0, rows, :] = dot(feat[rows, :], w_neigh[...]).astype(BF16)
        for i, dst, dev in own_sends:
            fcopy(i, 0, dst, ch, dev).start()

    loop(CHUNKS, project)

    devs = (
        at(0, core),
        at(0, other),
        at(-sgn, core),
        at(-2 * sgn, core),
        at(2 * sgn, core),
        at(-sgn, other),
        at(2 * (2 * core - 1), other),
        at(sgn, core),
        at(sgn, other),
    )
    for b, dev in enumerate(devs):
        tab[b] = dev
    slots = tiles.shape[0]

    def densify(b):
        for t in range(2):
            column = tab[b] * 2 + t

            def seek(j, found):
                return jnp.maximum(found, jnp.where(blist[j, 1] == column, j, 0))

            slot = lax.fori_loop(0, slots, seek, 0)
            target = blist[slot, 0] - 2 * row
            live = slot < bcount[0]
            block = tiles[slot]
            flipped = block.T
            for r in range(2):
                take = jnp.logical_and(live, target == r)
                here = pl.ds(r * tile, tile)
                there = pl.ds(t * tile, tile)
                dense[b, here, there] = jnp.where(take, block, jnp.zeros_like(block))
                dense_t[b, there, here] = jnp.where(take, flipped, jnp.zeros_like(flipped))

    def add_block(b):
        acc[...] += dot(dense[b], win[b])

    def relay(ch):
        fwait(3, ch)
        fcopy(4, 3, 7, ch, ypair).start()
        fwait(2, ch)
        fcopy(5, 2, 5, ch, partner).start()
        fwait(4, ch)
        fcopy(6, far, 6, ch, partner).start()

    def densify_and_relay(ch):
        for i in range(4):
            densify(4 * ch + i)
        relay(ch)

    loop(CHUNKS, densify_and_relay)
    densify(NEAR - 1)

    acc[...] = dot(dense[0], win[0])

    feat_t[...] = feat[...].T

    def arrive(b):
        loop(CHUNKS, lambda ch: fwait(b, ch))
        add_block(b)

    arrive(1)
    add_block(2)
    add_block(3)
    add_block(4)
    arrive(5)
    arrive(6)

    def relay_on(ch):
        fwait(7, ch)
        fcopy(7, 7, 8, ch, partner).start()

    loop(CHUNKS, relay_on)
    add_block(7)
    arrive(8)

    bias_rows = 8

    def activate(ch, bias_sum):
        rows = rows_of(ch)
        per_node = 1.0 / degree[pl.ds(ch, 1), :].astype(F32)
        inverse = jnp.broadcast_to(per_node, (step, step)).T[:, :1]
        pre = dot(feat[rows, :], w_self[...]) + acc[rows, :] * inverse + bias[...]
        square = pre * pre
        t = jnp.tanh(TANH_SCALE * (pre + TANH_CUBE * (square * pre)))
        half = 0.5 * (1.0 + t)
        act_out[rows, :] = (pre * half).astype(BF16)
        slope = half + (0.5 * TANH_SCALE) * pre * (1.0 - t * t) * (1.0 + (3.0 * TANH_CUBE) * square)
        grad_pre = cot[rows, :].astype(F32) * slope
        gpre_b[rows, :] = grad_pre.astype(BF16)
        msg[rows, :] = (grad_pre * inverse).astype(BF16)
        return bias_sum + jnp.sum(
            grad_pre.reshape(step // bias_rows, bias_rows, grad_pre.shape[1]), axis=0
        )

    bias_sum = lax.fori_loop(0, CHUNKS, activate, jnp.zeros((bias_rows, acc.shape[1]), F32))

    def term(b, rows):
        return dot(dense_t[b, rows, :], msg[...])

    def lcopy(i, ch):
        rows = rows_of(ch)
        return rc(lane_out.at[i, rows], lane_in.at[i, rows], lsend.at[i, ch], lrecv.at[i, ch], partner)

    def ncopy(i, ch, dev):
        rows = rows_of(ch)
        return rc(net_out.at[i, rows], net_in.at[i, rows], nsend.at[i, ch], nrecv.at[i, ch], dev)

    def lane_term(i, b):
        def body(ch):
            rows = rows_of(ch)
            lane_out[i, rows, :] = term(b, rows).astype(BF16)
            lcopy(i, ch).start()

        return body

    loop(CHUNKS, lane_term(0, 8))
    loop(CHUNKS, lane_term(1, 6))

    def send_relay(ch):
        rows = rows_of(ch)
        mine = term(7, rows)
        lcopy(0, ch).wait_recv()
        net_out[0, rows, :] = (mine + lane_in[0, rows, :].astype(F32)).astype(BF16)
        ncopy(0, ch, ypair).start()

    loop(CHUNKS, send_relay)
    far_pos = (core != side).astype(F32)
    far_neg = 1.0 - far_pos

    def send_pos(ch):
        rows = rows_of(ch)
        mine = term(4, rows)
        lcopy(1, ch).wait_recv()
        net_out[1, rows, :] = (mine + far_pos * lane_in[1, rows, :].astype(F32)).astype(BF16)
        ncopy(1, ch, zpos).start()

    loop(CHUNKS, send_pos)
    loop(CHUNKS, lane_term(2, 5))

    def send_y(ch):
        rows = rows_of(ch)
        mine = term(2, rows)
        lcopy(2, ch).wait_recv()
        net_out[2, rows, :] = (mine + lane_in[2, rows, :].astype(F32)).astype(BF16)
        ncopy(2, ch, ypair).start()

    loop(CHUNKS, send_y)

    def send_neg(ch):
        rows = rows_of(ch)
        mine = term(3, rows) + far_neg * lane_in[1, rows, :].astype(F32)
        ncopy(0, ch, ypair).wait_recv()
        net_out[3, rows, :] = (mine + net_in[0, rows, :].astype(F32)).astype(BF16)
        ncopy(3, ch, zneg).start()

    loop(CHUNKS, send_neg)
    loop(CHUNKS, lane_term(3, 1))

    f_in = feat.shape[1]
    half_f, quarter_f = f_in // 2, f_in // 4

    width = gloc.shape[2]

    def reduce_stages():
        (s1, r1, s2, r2, s3, r3, gath, b_out, b_in, gs, gr, bs, br) = red
        depth = chips // 2
        piece_f = quarter_f // depth
        z = chip // 2
        my_half = pl.multiple_of(core * half_f, half_f)
        not_half = pl.multiple_of(other * half_f, half_f)
        my_quarter = pl.multiple_of(my_half + side * quarter_f, quarter_f)
        not_quarter = pl.multiple_of(my_half + (1 - side) * quarter_f, quarter_f)
        my_piece = pl.multiple_of(my_quarter + z * piece_f, piece_f)
        far_z = [lax.rem(z + j, depth) for j in range(1, depth)]

        def c1(g):
            return rc(s1.at[g], r1.at[g], gs.at[g, 0], gr.at[g, 0], partner)

        def c2(g):
            return rc(s2.at[g], r2.at[g], gs.at[g, 1], gr.at[g, 1], ypair)

        def c3(g, j):
            return rc(
                s3.at[g, j], r3.at[g, j], gs.at[g, 2 + j], gr.at[g, 2 + j], zline[j]
            )

        def c4(g, j):
            return rc(
                gath.at[g, 0, 0, 0],
                gath.at[g, 0, 0, j + 1],
                gs.at[g, 1 + depth + j],
                gr.at[g, 1 + depth + j],
                zline[j],
            )

        last = 2 * depth

        def c5(g):
            return rc(gath.at[g, 0, 0], gath.at[g, 0, 1], gs.at[g, last], gr.at[g, last], ypair)

        def c6(g):
            return rc(gath.at[g, 0], gath.at[g, 1], gs.at[g, last + 1], gr.at[g, last + 1], partner)

        def stage1(g):
            for a in range(2):
                start = not_half + (side if a == 0 else 1 - side) * quarter_f
                rows = pl.ds(pl.multiple_of(start, quarter_f), quarter_f)
                s1[g, a] = gloc[g, rows, :].astype(BF16)
            c1(g).start()

        def stage2(g):
            c1(g).wait_recv()
            s2[g] = (
                gloc[g, pl.ds(not_quarter, quarter_f), :]
                + r1[g, 1].astype(F32)
            ).astype(BF16)
            c2(g).start()

        def stage3(g):
            mine = (
                gloc[g, pl.ds(my_quarter, quarter_f), :]
                + r1[g, 0].astype(F32)
            )
            c2(g).wait_recv()
            mine = mine + r2[g].astype(F32)
            gloc[g, pl.ds(my_quarter, quarter_f), :] = mine
            for j in range(depth - 1):
                start = pl.multiple_of(my_quarter + far_z[j] * piece_f, piece_f)
                s3[g, j] = gloc[g, pl.ds(start, piece_f), :].astype(BF16)
            for j in range(depth - 1):
                c3(g, j).start()

        def stage4(g):
            total = gloc[g, pl.ds(my_piece, piece_f), :]
            for j in range(depth - 1):
                c3(g, j).wait_recv()
                total = total + r3[g, j].astype(F32)
            gath[g, 0, 0, 0] = total.astype(BF16)
            for j in range(depth - 1):
                c4(g, j).start()

        def stage5(g):
            for j in range(depth - 1):
                c4(g, j).wait_recv()
            c5(g).start()

        def stage6(g):
            c5(g).wait_recv()
            c6(g).start()

        def stage7(g):
            out = gself_out if g < 2 else gneigh_out
            cols = pl.ds(g % 2 * width, width)
            c6(g).wait_recv()
            for a in range(2):
                for b in range(2):
                    base = (core if a == 0 else other) * half_f
                    base = base + (side if b == 0 else 1 - side) * quarter_f
                    for j in range(depth):
                        start = base + lax.rem(z + depth - j, depth) * piece_f
                        rows = pl.ds(pl.multiple_of(start, piece_f), piece_f)
                        out[rows, cols] = gath[g, a, b, j]

        def bcopy(i, src, dev):
            return rc(b_out.at[src], b_in.at[i], bs.at[i], br.at[i], dev)

        def bias_start():
            b_out[0] = bias_sum
            bcopy(0, 0, partner).start()
            bcopy(0, 0, partner).wait_recv()
            b_out[1] = b_out[0] + b_in[0]
            bcopy(1, 1, ypair).start()
            bcopy(1, 1, ypair).wait_recv()
            b_out[2] = b_out[1] + b_in[1]
            for j in range(depth - 1):
                bcopy(2 + j, 2, zline[j]).start()

        def bias_end():
            total = b_out[2]
            for j in range(depth - 1):
                bcopy(2 + j, 2, zline[j]).wait_recv()
                total = total + b_in[2 + j]
            gbias_out[...] = jnp.sum(total, axis=0, keepdims=True)

        def settle():
            for g in range(4):
                c1(g).wait_send()
                c2(g).wait_send()
                for j in range(depth - 1):
                    c3(g, j).wait_send()
                    c4(g, j).wait_send()
                c5(g).wait_send()
                c6(g).wait_send()
            bcopy(0, 0, partner).wait_send()
            bcopy(1, 1, ypair).wait_send()
            for j in range(depth - 1):
                bcopy(2 + j, 2, zline[j]).wait_send()

        return (
            stage1, stage2, stage3, stage4, stage5, stage6, stage7, bias_start, bias_end, settle
        )

    def weight_grad(u, source):
        cols = pl.ds(u % 2 * width, width)

        gloc[u] = dot(feat_t[...], source[:, cols])

    weight_grad(0, gpre_b)
    if reduce_here:
        stages = reduce_stages()
        stage1, stage2, stage3, stage4, stage5, stage6, stage7, bias_start, bias_end, settle = stages
        stage1(0)
    weight_grad(1, gpre_b)
    if reduce_here:
        stage1(1)
        bias_start()
        stage2(0)
        stage2(1)

    def gather_own(ch):
        rows = rows_of(ch)
        total = term(0, rows)
        lcopy(3, ch).wait_recv()
        total = total + lane_in[3, rows, :].astype(F32)
        ncopy(2, ch, ypair).wait_recv()
        total = total + net_in[2, rows, :].astype(F32)
        ncopy(1, ch, zpos).wait_recv()
        total = total + net_in[1, rows, :].astype(F32)
        ncopy(3, ch, zneg).wait_recv()
        total = total + net_in[3, rows, :].astype(F32)
        msg_back[rows, :] = total.astype(BF16)

    msg_back = win.at[0]
    if reduce_here:
        stage3(0)
        stage3(1)
    for i, src, dst in ((0, 0, 3), (1, 0, 4), (2, 0, 2), (3, 0, 1), (4, 3, 7), (5, 2, 5), (6, 3, 6), (7, 7, 8)):
        loop(CHUNKS, lambda ch, i=i, src=src, dst=dst: fcopy(i, src, dst, ch, partner).wait_send())
    loop(CHUNKS, gather_own)

    def feature_grad(ch):
        rows = rows_of(ch)
        gfeat_out[rows, :] = (
            dot_nt(gpre_b[rows, :], w_self[...]) + dot_nt(msg_back[rows, :], w_neigh[...])
        ).astype(BF16)

    weight_grad(2, msg_back)
    if reduce_here:
        stage1(2)
    weight_grad(3, msg_back)
    if reduce_here:
        stage1(3)
        stage2(2)
        stage4(0)
        stage2(3)
        stage4(1)
        stage3(2)
        stage5(0)
        stage3(3)
        stage5(1)
        stage6(0)
        stage4(2)
        stage6(1)
        stage4(3)
        stage5(2)
        stage5(3)
    loop(CHUNKS, feature_grad)
    if reduce_here:
        stage6(2)
        stage6(3)
        stage7(0)
        stage7(1)
        bias_end()
        stage7(2)
        stage7(3)
        settle()
    else:
        for u in range(4):
            cols = pl.ds(u % 2 * width, width)
            out = gself_out if u < 2 else gneigh_out
            out[:, cols] = gloc[u]
        gbias_out[...] = jnp.sum(bias_sum, axis=0, keepdims=True)

    def drain(ch):
        for i in range(4):
            lcopy(i, ch).wait_send()
        for i, dev in enumerate((ypair, zpos, ypair, zneg)):
            ncopy(i, ch, dev).wait_send()

    loop(CHUNKS, drain)


def on_device(
    features, degree, block_list, block_count, tiles, self_weight, neigh_weight, bias, cotangent
):
    nodes, f_in = features.shape
    hid = neigh_weight.shape[1]
    n_row = lax.axis_size("row")
    depth = n_row // 4
    reduce_here = f_in % (4 * depth * 16) == 0 and depth >= 3 and depth <= 4
    vmem = pl.BlockSpec(memory_space=pltpu.VMEM)
    smem = pl.BlockSpec(memory_space=pltpu.SMEM)
    dma = pltpu.SemaphoreType.DMA
    block = (nodes, hid)
    scratch = [
        pltpu.VMEM((NEAR,) + block, BF16),
        pltpu.VMEM((NEAR, nodes, nodes), BF16),
        pltpu.VMEM((NEAR, nodes, nodes), BF16),
        pltpu.VMEM((f_in, nodes), BF16),
        pltpu.VMEM(block, F32),
        pltpu.VMEM(block, BF16),
        pltpu.VMEM(block, BF16),
        pltpu.VMEM((4,) + block, BF16),
        pltpu.VMEM((4,) + block, BF16),
        pltpu.VMEM((4,) + block, BF16),
        pltpu.VMEM((4,) + block, BF16),
        pltpu.VMEM((4, f_in, hid // 2), F32),
        pltpu.SMEM((NEAR,), jnp.int32),
        dma((8, CHUNKS)),
        dma((NEAR, CHUNKS)),
        dma((4, CHUNKS)),
        dma((4, CHUNKS)),
        dma((4, CHUNKS)),
        dma((4, CHUNKS)),
    ]
    if reduce_here:
        quarter, wide = f_in // 4, hid // 2
        scratch += [
            pltpu.VMEM((4, 2, quarter, wide), BF16),
            pltpu.VMEM((4, 2, quarter, wide), BF16),
            pltpu.VMEM((4, quarter, wide), BF16),
            pltpu.VMEM((4, quarter, wide), BF16),
            pltpu.VMEM((4, depth - 1, quarter // depth, wide), BF16),
            pltpu.VMEM((4, depth - 1, quarter // depth, wide), BF16),
            pltpu.VMEM((4, 2, 2, depth, quarter // depth, wide), BF16),
            pltpu.VMEM((3, 8, hid), F32),
            pltpu.VMEM((1 + depth, 8, hid), F32),
            dma((4, 2 * depth + 2)),
            dma((4, 2 * depth + 2)),
            dma((1 + depth,)),
            dma((1 + depth,)),
        ]
    act, gfeat, gself, gneigh, gbias = pl.pallas_call(
        functools.partial(kernel, n_row, reduce_here),
        out_shape=(
            jax.ShapeDtypeStruct(block, BF16),
            jax.ShapeDtypeStruct((nodes, f_in), BF16),
            jax.ShapeDtypeStruct((f_in, hid), BF16 if reduce_here else F32),
            jax.ShapeDtypeStruct((f_in, hid), BF16 if reduce_here else F32),
            jax.ShapeDtypeStruct((1, hid), F32),
        ),
        in_specs=[vmem, vmem, smem, smem, vmem, vmem, vmem, vmem, vmem],
        out_specs=(vmem,) * 5,
        scratch_shapes=scratch,
        compiler_params=pltpu.CompilerParams(
            collective_id=0, has_side_effects=True, vmem_limit_bytes=60 * 1024 * 1024
        ),
    )(
        features,
        degree.reshape(CHUNKS, nodes // CHUNKS),
        block_list,
        block_count,
        tiles,
        self_weight,
        neigh_weight,
        bias.reshape(1, hid),
        cotangent,
    )
    gbias = gbias.reshape(hid)
    gself, gneigh = gself.astype(F32), gneigh.astype(F32)
    if not reduce_here:
        gself, gneigh, gbias = lax.psum((gself, gneigh, gbias), "row")
    return act, gfeat, gself, gneigh, gbias


def solution(mesh):
    return jax.shard_map(
        on_device,
        mesh=mesh,
        in_specs=(
            P(("grp", "row"), None),
            P(("grp", "row")),
            P(("grp", "row"), None),
            P(("grp", "row")),
            P(("grp", "row"), None, None),
            P(),
            P(),
            P(),
            P(("grp", "row"), None),
        ),
        out_specs=(
            P(("grp", "row"), None),
            P(("grp", "row"), None),
            P("grp", None),
            P("grp", None),
            P("grp"),
        ),
        check_vma=False,
    )
```
